32 devices in a mesh: tensor: 8 (over z, y), context: 4 (over x, core).
Axes of the slice: x: 2, y: 2, z: 4, core: 2. Of those that a mesh axis runs over, the one named last changes fastest.
Arguments:
- tokens: bfloat16 [1536, 8192], P('context'), may hold values from -48 to 48
- w_query: bfloat16 [8192, 1024], P(None, 'tensor'), may hold values from -0.0625 to 0.0625
- w_key: bfloat16 [8192, 1024], P(None, 'tensor'), may hold values from -0.0625 to 0.0625
- w_value: bfloat16 [8192, 1024], P(None, 'tensor'), may hold values from -0.0625 to 0.0625
- mix_gate: bfloat16 [8, 16], replicated, may hold values from -2 to 2
- mix_up: bfloat16 [8, 16], replicated, may hold values from -2 to 2
- mix_down: bfloat16 [16, 8], replicated, may hold values from -1.5 to 1.5
- block_ids: int32 [16], P('context'), may hold values from 0 to 7, as said below
Outputs:
- attended: bfloat16 [1536, 1024], P('context', 'tensor')
The draws below stay inside these ranges and needn't reach their ends.
Inputs may be any that keep to these rules, and one draw needn't show every extreme that they name: `block_ids`: device c of the context axis holds entries 4c to 4c+3: (a, 7 - a) for the first sequence and (b, 7 - b) for the second; over all devices each sequence's block numbers appear once each.
All inputs are finite; a program needn't handle non-finite values.
Results may differ from the reference program's by a relative error of at most 0.012.
The reference program's roundings to bfloat16 on the way (of `queries`, `hidden` and `mixed`) count: a program that leaves them out, or rounds other values in their place, can miss the bound.
Values may be sent and summed in bfloat16 or wider, within the bound.
A program may use at most 64 MiB of HBM per device.

```python
import jax
import jax.numpy as jnp
from jax import lax

D = 8192
HEAD_DIM = 128
BLK = 96
HEADS = 8
MIXF = 16
TOKENS = 1536
N_CONTEXT = 4


def draw_tokens(key, part):
    base = jax.random.truncated_normal(key, -6.0, 6.0, (TOKENS, D), jnp.float32)
    return base.astype(jnp.bfloat16)


def draw_block_ids(key, part):
    firsts = jnp.stack([jax.random.permutation(jax.random.fold_in(key, 11 + s), N_CONTEXT) for s in range(2)], axis=1)
    firsts = firsts.astype(jnp.int32)
    paired = jnp.stack([firsts, 2 * N_CONTEXT - 1 - firsts], axis=2)
    return paired.reshape(4 * N_CONTEXT).astype(jnp.int32)


def block_scale(rng, extent, cuts, smallest, high):
    loudness, own = 1.0, jax.random.fold_in(rng, 6)
    for axis_at, parts in cuts:
        heights = jnp.exp(jax.random.uniform(jax.random.fold_in(own, axis_at), (parts,), jnp.float32, smallest / len(cuts), high / len(cuts)))
        loudness = loudness * jnp.repeat(heights, extent[axis_at] // parts).reshape([-1 if axis == axis_at else 1 for axis in range(len(extent))])
    return loudness


def gaussian(key, dims, scale, most, shards=(), kind=jnp.bfloat16):
    level = block_scale(key, dims, shards, -0.22, 0.18) if shards else 1.0
    values = jax.random.normal(key, dims, jnp.float32) * scale * level
    return jnp.minimum(jnp.maximum(values, -most), most).astype(kind)


def setup_inputs(seed: int = 0) -> dict:
    arg_keys = jax.random.split(jax.random.key(seed), 9)
    tokens = draw_tokens(jax.random.fold_in(arg_keys[8], 71), 0)
    w_query = gaussian(arg_keys[1], (D, HEADS * HEAD_DIM), D ** -0.5, 0.0625, ((1, 8),))
    w_key = gaussian(arg_keys[2], (D, HEADS * HEAD_DIM), D ** -0.5, 0.0625, ((1, 8),))
    w_value = gaussian(arg_keys[3], (D, HEADS * HEAD_DIM), D ** -0.5, 0.0625, ((1, 8),))
    mix_gate = gaussian(arg_keys[4], (HEADS, MIXF), HEADS ** -0.5, 2.0)
    mix_up = gaussian(arg_keys[5], (HEADS, MIXF), HEADS ** -0.5, 2.0)
    mix_down = gaussian(arg_keys[6], (MIXF, HEADS), MIXF ** -0.5, 1.5)
    block_ids = draw_block_ids(jax.random.fold_in(arg_keys[8], 71), 0)
    return dict(tokens=tokens, w_query=w_query, w_key=w_key, w_value=w_value, mix_gate=mix_gate, mix_up=mix_up, mix_down=mix_down, block_ids=block_ids)


def reference(tokens, w_query, w_key, w_value, mix_gate, mix_up, mix_down, block_ids):
    row_index = jnp.arange(TOKENS, dtype=jnp.int32)
    block_of = row_index // BLK
    positions = jnp.take(block_ids, block_of).astype(jnp.int32) * BLK + row_index % BLK
    seq_index = (block_of % 4) // 2
    queries = jnp.dot(tokens, w_query, preferred_element_type=jnp.float32).astype(jnp.bfloat16).reshape(TOKENS, HEADS, HEAD_DIM)
    keys_all = jnp.dot(tokens, w_key, preferred_element_type=jnp.float32).astype(jnp.bfloat16).reshape(TOKENS, HEADS, HEAD_DIM)
    values_all = jnp.dot(tokens, w_value, preferred_element_type=jnp.float32).astype(jnp.bfloat16).reshape(TOKENS, HEADS, HEAD_DIM)
    value_float = values_all.astype(jnp.float32)
    gate_part = jnp.einsum("thc,hf->tcf", value_float, mix_gate.astype(jnp.float32))
    up_part = jnp.einsum("thc,hf->tcf", value_float, mix_up.astype(jnp.float32))
    hidden = (jax.nn.silu(gate_part) * up_part).astype(jnp.bfloat16)
    mixing = jnp.einsum("tcf,fh->thc", hidden.astype(jnp.float32), mix_down.astype(jnp.float32))
    mixed = (value_float + mixing).astype(jnp.bfloat16)
    allowed = (seq_index[:, None] == seq_index[None, :]) & (positions[None, :] <= positions[:, None])
    scale = HEAD_DIM ** -0.5

    def one_head(operands):
        q_head, k_head, v_head = operands
        scores = jnp.dot(q_head, k_head.T, preferred_element_type=jnp.float32) * scale
        scores = jnp.where(allowed, scores, -1e30)
        top = jnp.max(scores, axis=1, keepdims=True)
        weights = jnp.where(allowed, jnp.exp(scores - top), 0.0)
        total = jnp.sum(weights, axis=1, keepdims=True)
        summed = jnp.dot(weights.astype(jnp.bfloat16), v_head, preferred_element_type=jnp.float32)
        return (summed / total).astype(jnp.bfloat16)

    heads_out = lax.map(one_head, (queries.transpose(1, 0, 2), keys_all.transpose(1, 0, 2), mixed.transpose(1, 0, 2)))
    return heads_out.transpose(1, 0, 2).reshape(TOKENS, HEADS * HEAD_DIM)
```

```python
import functools

import jax
import jax.numpy as jnp
from jax import lax
from jax.experimental import pallas as pl
from jax.experimental.pallas import tpu as pltpu
from jax.sharding import PartitionSpec as P

HEAD_DIM = 128
BLK = 96
SEQS = 2
MESH = pl.DeviceIdType.MESH
F32 = jnp.float32
BF16 = jnp.bfloat16


def flat_rows(x):
    rows = x.size // x.shape[-1]
    if x.shape[-2] % 16:
        return x.astype(F32).reshape(rows, x.shape[-1]).astype(x.dtype)
    return x.reshape(rows, x.shape[-1])


def picks(shape, row_div, col_div):
    row = lax.broadcasted_iota(jnp.int32, shape, 0) // row_div
    col = lax.broadcasted_iota(jnp.int32, shape, 1) // col_div
    return (row == col).astype(F32)


def spread(small, step):
    tall, wide = small.shape[0] * step, small.shape[1] * step
    lifted = jnp.dot(
        picks((tall, small.shape[0]), step, 1), small, preferred_element_type=F32
    )
    lifted = jnp.dot(
        lifted, picks((small.shape[1], wide), 1, step), preferred_element_type=F32
    )
    row = lax.broadcasted_iota(jnp.int32, (tall, wide), 0) % step
    col = lax.broadcasted_iota(jnp.int32, (tall, wide), 1) % step
    return jnp.where(row == col, lifted, 0.0).astype(BF16)


def kernel(
    heads, ctx, parts,
    ids_ref, x_ref, wq_ref, wk_ref, wv_ref, gate_ref, up_ref, down_ref, out_ref,
    xbuf, wvbuf, wkqbuf, gubuf, dnbuf, vsend, vrecv, msend, mbuf, kbuf, qbuf, idbuf, pbuf, tbuf,
    load_sem, vs_sem, vr_sem, ms_sem, mr_sem, ks_sem, kr_sem, is_sem, ir_sem, cs_sem, cr_sem,
):
    ti = lax.axis_index("tensor")
    ci = lax.axis_index("context")
    rows, depth = x_ref.shape
    step = depth // parts
    slab = rows // heads
    seq_rows = rows // SEQS

    loads = []

    def load(src, dst):
        copy = pltpu.make_async_copy(src, dst, load_sem.at[len(loads)])
        copy.start()
        loads.append(copy)
        return copy

    v_loads, kq_loads = [], []
    for i in range(parts):
        ks = pl.ds(i * step, step)
        v_loads.append(
            (load(x_ref.at[:, ks], xbuf.at[:, ks]), load(wv_ref.at[ks, :], wvbuf.at[ks, :]))
        )
    for i in range(parts):
        ks = pl.ds(i * step, step)
        kq_loads.append(
            (
                load(wk_ref.at[ks, :], wkqbuf.at[ks, 0:HEAD_DIM]),
                load(wq_ref.at[ks, :], wkqbuf.at[ks, HEAD_DIM : 2 * HEAD_DIM]),
            )
        )

    barrier = pltpu.get_barrier_semaphore()
    for d in range(1, heads):
        pl.semaphore_signal(
            barrier, inc=1, device_id={"tensor": lax.rem(ti + d, heads)}, device_id_type=MESH
        )
    for d in range(1, ctx):
        pl.semaphore_signal(
            barrier, inc=1, device_id={"context": lax.rem(ci + d, ctx)}, device_id_type=MESH
        )

    tile = 16 if slab % 16 == 0 else slab
    half = gate_ref.shape[1] * tile
    gubuf[0:half] = spread(gate_ref[...].astype(F32).T, tile)
    gubuf[half : 2 * half] = spread(up_ref[...].astype(F32).T, tile)
    dnbuf[...] = spread(down_ref[...].astype(F32).T, tile)

    sub = lax.broadcasted_iota(jnp.int32, (8, 128), 0)
    own_ids = jnp.zeros((8, 128), jnp.int32)
    for b in range(2 * SEQS):
        own_ids = jnp.where(sub == b, ids_ref[b], own_ids)
    idbuf[ci] = own_ids

    acc = jnp.zeros((rows, HEAD_DIM), F32)
    for i in range(parts):
        for copy in v_loads[i]:
            copy.wait()
        ks = slice(i * step, (i + 1) * step)
        acc += jnp.dot(xbuf[:, ks], wvbuf[ks, :], preferred_element_type=F32)
    if slab % 16:
        vsend[...] = acc.reshape(heads, slab, HEAD_DIM).astype(BF16)
    else:
        vsend[...] = acc.astype(BF16).reshape(heads, slab, HEAD_DIM)

    pl.semaphore_wait(barrier, heads - 1 + ctx - 1)

    v_copies = []
    for d in range(1, heads):
        peer = lax.rem(ti + d, heads)
        copy = pltpu.make_async_remote_copy(
            src_ref=vsend.at[peer], dst_ref=vrecv.at[ti],
            send_sem=vs_sem.at[d], recv_sem=vr_sem.at[ti],
            device_id={"tensor": peer}, device_id_type=MESH,
        )
        copy.start()
        v_copies.append(copy)
    i_copies = []
    for d in range(1, ctx):
        peer = lax.rem(ci + d, ctx)
        copy = pltpu.make_async_remote_copy(
            src_ref=idbuf.at[ci], dst_ref=idbuf.at[ci],
            send_sem=is_sem.at[d], recv_sem=ir_sem.at[ci],
            device_id={"context": peer}, device_id_type=MESH,
        )
        copy.start()
        i_copies.append(copy)
    vrecv[ti] = vsend[ti]

    acc = jnp.zeros((rows, 2 * HEAD_DIM), F32)
    for i in range(parts):
        for copy in kq_loads[i]:
            copy.wait()
        ks = slice(i * step, (i + 1) * step)
        acc += jnp.dot(xbuf[:, ks], wkqbuf[ks, :], preferred_element_type=F32)
    kbuf[ci] = acc[:, :HEAD_DIM].astype(BF16).reshape(SEQS, seq_rows, HEAD_DIM)
    k_copies = []
    for d in range(1, ctx):
        peer = lax.rem(ci + d, ctx)
        copy = pltpu.make_async_remote_copy(
            src_ref=kbuf.at[ci], dst_ref=kbuf.at[ci],
            send_sem=ks_sem.at[d], recv_sem=kr_sem.at[ci],
            device_id={"context": peer}, device_id_type=MESH,
        )
        copy.start()
        k_copies.append(copy)
    qbuf[...] = acc[:, HEAD_DIM:].astype(BF16)

    for d in range(1, heads):
        src = lax.rem(ti + d, heads)
        pltpu.make_async_remote_copy(
            src_ref=vsend.at[src], dst_ref=vrecv.at[src],
            send_sem=vs_sem.at[d], recv_sem=vr_sem.at[src],
            device_id={"tensor": src}, device_id_type=MESH,
        ).wait_recv()
    pieces = slab // tile
    x = jnp.concatenate(
        [flat_rows(vrecv[:, j * tile : (j + 1) * tile, :]) for j in range(pieces)], axis=1
    )
    both = jnp.dot(gubuf[...], x, preferred_element_type=F32)
    hidden = (jax.nn.silu(both[:half]) * both[half:]).astype(BF16)
    mixed = x.astype(F32) + jnp.dot(dnbuf[...], hidden, preferred_element_type=F32)
    for j in range(pieces):
        piece = mixed[:, j * HEAD_DIM : (j + 1) * HEAD_DIM]
        if tile % 16:
            piece = piece.reshape(heads, tile, HEAD_DIM).astype(BF16)
        else:
            piece = piece.astype(BF16).reshape(heads, tile, HEAD_DIM)
        msend[:, j * tile : (j + 1) * tile, :] = piece
    m_copies = []
    for d in range(1, heads):
        peer = lax.rem(ti + d, heads)
        copy = pltpu.make_async_remote_copy(
            src_ref=msend.at[peer], dst_ref=mbuf.at[ci, ti],
            send_sem=ms_sem.at[d], recv_sem=mr_sem.at[ti],
            device_id={"tensor": peer}, device_id_type=MESH,
        )
        copy.start()
        m_copies.append(copy)
    mbuf[ci, ti] = msend[ti]

    for d in range(1, ctx):
        src = lax.rem(ci + d, ctx)
        pltpu.make_async_remote_copy(
            src_ref=idbuf.at[src], dst_ref=idbuf.at[src],
            send_sem=is_sem.at[d], recv_sem=ir_sem.at[src],
            device_id={"context": src}, device_id_type=MESH,
        ).wait_recv()
    for d in range(1, ctx):
        src = lax.rem(ci + d, ctx)
        pltpu.make_async_remote_copy(
            src_ref=kbuf.at[src], dst_ref=kbuf.at[src],
            send_sem=ks_sem.at[d], recv_sem=kr_sem.at[src],
            device_id={"context": src}, device_id_type=MESH,
        ).wait_recv()
    scale = HEAD_DIM ** (-0.5)
    count = ctx * seq_rows
    lane = lax.broadcasted_iota(jnp.int32, (1, count), 1)
    row = lax.broadcasted_iota(jnp.int32, (seq_rows, 1), 0)
    for s in range(SEQS):
        key_pos = jnp.zeros((1, count), jnp.int32)
        for c in range(ctx):
            ids = idbuf[c]
            for b in range(2):
                r = 2 * s + b
                wide = jnp.concatenate([ids[r : r + 1, :]] * (count // 128), axis=1)
                key_pos = jnp.where(lane // BLK == 2 * c + b, wide, key_pos)
        key_pos = key_pos * BLK + lane % BLK
        query_pos = (
            jnp.where(row < BLK, ids_ref[2 * s], ids_ref[2 * s + 1]) * BLK + row % BLK
        )
        keys = kbuf[:, s].reshape(count, HEAD_DIM)
        scores = lax.dot_general(
            qbuf[s * seq_rows : (s + 1) * seq_rows, :], keys,
            (((1,), (1,)), ((), ())), preferred_element_type=F32,
        ) * scale
        scores = jnp.where(key_pos <= query_pos, scores, -1e30)
        weights = jnp.exp(scores - jnp.max(scores, axis=1, keepdims=True))
        tbuf[s] = jnp.broadcast_to(jnp.sum(weights, axis=1, keepdims=True), (seq_rows, HEAD_DIM))
        pbuf[s] = weights.astype(BF16)

    for d in range(1, heads):
        src = lax.rem(ti + d, heads)
        pltpu.make_async_remote_copy(
            src_ref=msend.at[src], dst_ref=mbuf.at[ci, src],
            send_sem=ms_sem.at[d], recv_sem=mr_sem.at[src],
            device_id={"tensor": src}, device_id_type=MESH,
        ).wait_recv()
    c_copies = []
    for d in range(1, ctx):
        peer = lax.rem(ci + d, ctx)
        copy = pltpu.make_async_remote_copy(
            src_ref=mbuf.at[ci], dst_ref=mbuf.at[ci],
            send_sem=cs_sem.at[d], recv_sem=cr_sem.at[ci],
            device_id={"context": peer}, device_id_type=MESH,
        )
        copy.start()
        c_copies.append(copy)
    for d in range(1, ctx):
        src = lax.rem(ci + d, ctx)
        pltpu.make_async_remote_copy(
            src_ref=mbuf.at[src], dst_ref=mbuf.at[src],
            send_sem=cs_sem.at[d], recv_sem=cr_sem.at[src],
            device_id={"context": src}, device_id_type=MESH,
        ).wait_recv()
    per_seq = heads // SEQS
    for s in range(SEQS):
        values = flat_rows(mbuf[:, s * per_seq : (s + 1) * per_seq])
        summed = jnp.dot(pbuf[s], values, preferred_element_type=F32)
        out_ref[s * seq_rows : (s + 1) * seq_rows, :] = (summed / tbuf[s]).astype(BF16)

    for copy in v_copies + i_copies + k_copies + m_copies + c_copies:
        copy.wait_send()


def solution(mesh):
    heads, ctx = mesh.shape["tensor"], mesh.shape["context"]

    def shards(tokens, w_query, w_key, w_value, mix_gate, mix_up, mix_down, block_ids):
        rows, depth = tokens.shape
        slab = rows // heads
        seq_rows = rows // SEQS
        tile = 16 if slab % 16 == 0 else slab
        mixf = mix_gate.shape[1]
        parts = 8
        dma = pltpu.SemaphoreType.DMA
        vmem = pl.BlockSpec(memory_space=pltpu.VMEM)
        hbm = pl.BlockSpec(memory_space=pl.ANY)
        return pl.pallas_call(
            functools.partial(kernel, heads, ctx, parts),
            out_shape=jax.ShapeDtypeStruct((rows, HEAD_DIM), BF16),
            in_specs=[pl.BlockSpec(memory_space=pltpu.SMEM)] + [hbm] * 4 + [vmem] * 3,
            out_specs=vmem,
            scratch_shapes=[
                pltpu.VMEM((rows, depth), BF16),
                pltpu.VMEM((depth, HEAD_DIM), BF16),
                pltpu.VMEM((depth, 2 * HEAD_DIM), BF16),
                pltpu.VMEM((2 * mixf * tile, heads * tile), BF16),
                pltpu.VMEM((heads * tile, mixf * tile), BF16),
                pltpu.VMEM((heads, slab, HEAD_DIM), BF16),
                pltpu.VMEM((heads, slab, HEAD_DIM), BF16),
                pltpu.VMEM((heads, slab, HEAD_DIM), BF16),
                pltpu.VMEM((ctx, heads, slab, HEAD_DIM), BF16),
                pltpu.VMEM((ctx, SEQS, seq_rows, HEAD_DIM), BF16),
                pltpu.VMEM((rows, HEAD_DIM), BF16),
                pltpu.VMEM((ctx, 8, 128), jnp.int32),
                pltpu.VMEM((SEQS, seq_rows, ctx * seq_rows), BF16),
                pltpu.VMEM((SEQS, seq_rows, HEAD_DIM), F32),
                dma((4 * parts,)),
                dma((heads,)), dma((heads,)), dma((heads,)), dma((heads,)),
                dma((ctx,)), dma((ctx,)), dma((ctx,)), dma((ctx,)), dma((ctx,)), dma((ctx,)),
            ],
            compiler_params=pltpu.CompilerParams(
                collective_id=0, has_side_effects=True, vmem_limit_bytes=48 * 2**20
            ),
        )(block_ids, tokens, w_query, w_key, w_value, mix_gate, mix_up, mix_down)

    in_specs = (
        P("context", None),
        P(None, "tensor"),
        P(None, "tensor"),
        P(None, "tensor"),
        P(),
        P(),
        P(),
        P("context"),
    )
    out_specs = P("context", "tensor")
    return jax.shard_map(shards, mesh=mesh, in_specs=in_specs, out_specs=out_specs, check_vma=False)
```

```python
import functools

import jax
import jax.numpy as jnp
from jax import lax
from jax.experimental import pallas as pl
from jax.experimental.pallas import tpu as pltpu
from jax.sharding import PartitionSpec as P

HEAD_DIM = 128
BLK = 96
SEQS = 2
MESH = pl.DeviceIdType.MESH
F32 = jnp.float32
BF16 = jnp.bfloat16


def flat_rows(x):
    rows = x.size // x.shape[-1]
    if x.shape[-2] % 16:
        return x.astype(F32).reshape(rows, x.shape[-1]).astype(x.dtype)
    return x.reshape(rows, x.shape[-1])


def picks(shape, row_div, col_div):
    row = lax.broadcasted_iota(jnp.int32, shape, 0) // row_div
    col = lax.broadcasted_iota(jnp.int32, shape, 1) // col_div
    return (row == col).astype(F32)


def spread(small, step):
    tall, wide = small.shape[0] * step, small.shape[1] * step
    lifted = jnp.dot(
        picks((tall, small.shape[0]), step, 1), small, preferred_element_type=F32
    )
    lifted = jnp.dot(
        lifted, picks((small.shape[1], wide), 1, step), preferred_element_type=F32
    )
    row = lax.broadcasted_iota(jnp.int32, (tall, wide), 0) % step
    col = lax.broadcasted_iota(jnp.int32, (tall, wide), 1) % step
    return jnp.where(row == col, lifted, 0.0).astype(BF16)


def kernel(
    heads, ctx, parts,
    ids_hbm, x_ref, wq_ref, wk_ref, wv_ref, gate_hbm, up_hbm, down_hbm, out_ref,
    ids_ref, gate_ref, up_ref, down_ref,
    xbuf, wvbuf, wkqbuf, gubuf, dnbuf, vsend, vrecv, msend, mbuf, kbuf, qbuf, idbuf, pbuf, tbuf,
    load_sem, vs_sem, vr_sem, ms_sem, mr_sem, ks_sem, kr_sem, is_sem, ir_sem, cs_sem, cr_sem,
):
    ti = lax.axis_index("tensor")
    ci = lax.axis_index("context")
    rows, depth = x_ref.shape
    step = depth // parts
    slab = rows // heads
    seq_rows = rows // SEQS

    pairs = ctx // 2
    sib = ci + 1 - 2 * lax.rem(ci, 2)

    def far(d):
        return lax.rem(ci + 2 * d, ctx)

    def share(ref, peer, send, recv):
        copy = pltpu.make_async_remote_copy(
            src_ref=ref, dst_ref=ref, send_sem=send, recv_sem=recv,
            device_id={"context": peer}, device_id_type=MESH,
        )
        copy.start()
        return copy

    def arrived(ref, recv):
        pltpu.make_async_remote_copy(
            src_ref=ref, dst_ref=ref, send_sem=ks_sem.at[0], recv_sem=recv,
            device_id={"context": sib}, device_id_type=MESH,
        ).wait_recv()

    loads = []

    def load(src, dst):
        copy = pltpu.make_async_copy(src, dst, load_sem.at[len(loads)])
        copy.start()
        loads.append(copy)
        return copy

    small_loads = [
        load(gate_hbm, gate_ref), load(up_hbm, up_ref), load(down_hbm, down_ref), load(ids_hbm, ids_ref)
    ]
    v_loads, kq_loads = [], []
    for i in range(parts):
        ks = pl.ds(i * step, step)
        v_loads.append(
            (load(x_ref.at[:, ks], xbuf.at[:, ks]), load(wv_ref.at[ks, :], wvbuf.at[ks, :]))
        )
    for i in range(parts):
        ks = pl.ds(i * step, step)
        kq_loads.append(
            (
                load(wk_ref.at[ks, :], wkqbuf.at[ks, 0:HEAD_DIM]),
                load(wq_ref.at[ks, :], wkqbuf.at[ks, HEAD_DIM : 2 * HEAD_DIM]),
            )
        )

    barrier = pltpu.get_barrier_semaphore()
    for d in range(1, heads):
        pl.semaphore_signal(
            barrier, inc=1, device_id={"tensor": lax.rem(ti + d, heads)}, device_id_type=MESH
        )
    for d in range(1, ctx):
        pl.semaphore_signal(
            barrier, inc=1, device_id={"context": lax.rem(ci + d, ctx)}, device_id_type=MESH
        )

    for copy in small_loads:
        copy.wait()

    tile = 16 if slab % 16 == 0 else slab
    half = gate_ref.shape[1] * tile
    gubuf[0:half] = spread(gate_ref[...].astype(F32).T, tile)
    gubuf[half : 2 * half] = spread(up_ref[...].astype(F32).T, tile)
    dnbuf[...] = spread(down_ref[...].astype(F32), tile)

    sub = lax.broadcasted_iota(jnp.int32, (8, 128), 0)
    own_ids = jnp.zeros((8, 128), jnp.int32)
    for b in range(2 * SEQS):
        own_ids = jnp.where(sub == b, ids_ref[b], own_ids)
    idbuf[ci] = own_ids

    acc = jnp.zeros((rows, HEAD_DIM), F32)
    for i in range(parts):
        for copy in v_loads[i]:
            copy.wait()
        ks = slice(i * step, (i + 1) * step)
        acc += jnp.dot(xbuf[:, ks], wvbuf[ks, :], preferred_element_type=F32)
    if slab % 16:
        vsend[...] = acc.reshape(heads, slab, HEAD_DIM).astype(BF16)
    else:
        vsend[...] = acc.astype(BF16).reshape(heads, slab, HEAD_DIM)

    pl.semaphore_wait(barrier, heads - 1 + ctx - 1)

    v_copies = []
    for d in range(1, heads):
        peer = lax.rem(ti + d, heads)
        copy = pltpu.make_async_remote_copy(
            src_ref=vsend.at[peer], dst_ref=vrecv.at[ti],
            send_sem=vs_sem.at[d], recv_sem=vr_sem.at[ti],
            device_id={"tensor": peer}, device_id_type=MESH,
        )
        copy.start()
        v_copies.append(copy)
    i_copies = []
    for d in range(1, ctx):
        peer = lax.rem(ci + d, ctx)
        copy = pltpu.make_async_remote_copy(
            src_ref=idbuf.at[ci], dst_ref=idbuf.at[ci],
            send_sem=is_sem.at[d], recv_sem=ir_sem.at[ci],
            device_id={"context": peer}, device_id_type=MESH,
        )
        copy.start()
        i_copies.append(copy)
    vrecv[ti] = vsend[ti]

    acc = jnp.zeros((rows, 2 * HEAD_DIM), F32)
    for i in range(parts):
        for copy in kq_loads[i]:
            copy.wait()
        ks = slice(i * step, (i + 1) * step)
        acc += jnp.dot(xbuf[:, ks], wkqbuf[ks, :], preferred_element_type=F32)
    kbuf[ci] = acc[:, :HEAD_DIM].astype(BF16).reshape(SEQS, seq_rows, HEAD_DIM)
    k_copies = [share(kbuf.at[ci], sib, ks_sem.at[0], kr_sem.at[ci])]
    for d in range(1, pairs):
        k_copies.append(share(kbuf.at[ci], far(d), ks_sem.at[d], kr_sem.at[ci]))
    qbuf[...] = acc[:, HEAD_DIM:].astype(BF16)

    for d in range(1, heads):
        src = lax.rem(ti + d, heads)
        pltpu.make_async_remote_copy(
            src_ref=vsend.at[src], dst_ref=vrecv.at[src],
            send_sem=vs_sem.at[d], recv_sem=vr_sem.at[src],
            device_id={"tensor": src}, device_id_type=MESH,
        ).wait_recv()
    pieces = slab // tile
    x = jnp.concatenate(
        [flat_rows(vrecv[:, j * tile : (j + 1) * tile, :]) for j in range(pieces)], axis=1
    )
    both = jnp.dot(gubuf[...], x, preferred_element_type=F32)
    hidden = (jax.nn.silu(both[:half]) * both[half:]).astype(BF16)
    mixed = x.astype(F32) + jnp.dot(dnbuf[...], hidden, preferred_element_type=F32)
    for j in range(pieces):
        piece = mixed[:, j * HEAD_DIM : (j + 1) * HEAD_DIM]
        if tile % 16:
            piece = piece.reshape(heads, tile, HEAD_DIM).astype(BF16)
        else:
            piece = piece.astype(BF16).reshape(heads, tile, HEAD_DIM)
        msend[:, j * tile : (j + 1) * tile, :] = piece
    m_copies = []
    for d in range(1, heads):
        peer = lax.rem(ti + d, heads)
        copy = pltpu.make_async_remote_copy(
            src_ref=msend.at[peer], dst_ref=mbuf.at[ci, ti],
            send_sem=ms_sem.at[d], recv_sem=mr_sem.at[ti],
            device_id={"tensor": peer}, device_id_type=MESH,
        )
        copy.start()
        m_copies.append(copy)
    mbuf[ci, ti] = msend[ti]

    for d in range(1, pairs):
        arrived(kbuf.at[far(d)], kr_sem.at[far(d)])
        k_copies.append(share(kbuf.at[far(d)], sib, ks_sem.at[pairs - 1 + d], kr_sem.at[far(d)]))

    per_seq = heads // SEQS
    halves = [pl.ds(s * per_seq, per_seq) for s in range(SEQS)]
    c_copies = []
    for s in range(SEQS):
        for p in range(s * per_seq, (s + 1) * per_seq):

            @pl.when(p != ti)
            def _(p=p):
                pltpu.make_async_remote_copy(
                    src_ref=msend.at[p], dst_ref=mbuf.at[ci, p],
                    send_sem=ms_sem.at[0], recv_sem=mr_sem.at[p],
                    device_id={"tensor": p}, device_id_type=MESH,
                ).wait_recv()

        own = mbuf.at[ci, halves[s]]
        for d in range(1, pairs):
            c_copies.append(share(own, far(d), cs_sem.at[s, d], cr_sem.at[s, ci]))
        c_copies.append(share(own, sib, cs_sem.at[s, 0], cr_sem.at[s, ci]))

    for d in range(1, ctx):
        src = lax.rem(ci + d, ctx)
        arrived(idbuf.at[src], ir_sem.at[src])
    arrived(kbuf.at[sib], kr_sem.at[sib])
    for d in range(1, pairs):
        there = lax.rem(sib + 2 * d, ctx)
        arrived(kbuf.at[there], kr_sem.at[there])
    scale = HEAD_DIM ** (-0.5)
    count = ctx * seq_rows
    lane = lax.broadcasted_iota(jnp.int32, (1, count), 1)
    row = lax.broadcasted_iota(jnp.int32, (seq_rows, 1), 0)
    for s in range(SEQS):
        key_pos = jnp.zeros((1, count), jnp.int32)
        for c in range(ctx):
            ids = idbuf[c]
            for b in range(2):
                r = 2 * s + b
                wide = jnp.concatenate([ids[r : r + 1, :]] * (count // 128), axis=1)
                key_pos = jnp.where(lane // BLK == 2 * c + b, wide, key_pos)
        key_pos = key_pos * BLK + lane % BLK
        query_pos = (
            jnp.where(row < BLK, ids_ref[2 * s], ids_ref[2 * s + 1]) * BLK + row % BLK
        )
        keys = kbuf[:, s].reshape(count, HEAD_DIM)
        scores = lax.dot_general(
            qbuf[s * seq_rows : (s + 1) * seq_rows, :], keys,
            (((1,), (1,)), ((), ())), preferred_element_type=F32,
        ) * scale
        scores = jnp.where(key_pos <= query_pos, scores, -1e30)
        weights = jnp.exp(scores - jnp.max(scores, axis=1, keepdims=True))
        tbuf[s] = jnp.broadcast_to(jnp.sum(weights, axis=1, keepdims=True), (seq_rows, HEAD_DIM))
        pbuf[s] = weights.astype(BF16)

    for s in range(SEQS):
        for d in range(1, pairs):
            got = mbuf.at[far(d), halves[s]]
            arrived(got, cr_sem.at[s, far(d)])
            c_copies.append(share(got, sib, cs_sem.at[s, pairs - 1 + d], cr_sem.at[s, far(d)]))
    for s in range(SEQS):
        arrived(mbuf.at[sib, halves[s]], cr_sem.at[s, sib])
        for d in range(1, pairs):
            there = lax.rem(sib + 2 * d, ctx)
            arrived(mbuf.at[there, halves[s]], cr_sem.at[s, there])
        values = flat_rows(mbuf[:, s * per_seq : (s + 1) * per_seq])
        summed = jnp.dot(pbuf[s], values, preferred_element_type=F32)
        out_ref[s * seq_rows : (s + 1) * seq_rows, :] = (summed / tbuf[s]).astype(BF16)

    for copy in v_copies + i_copies + k_copies + m_copies + c_copies:
        copy.wait_send()


def solution(mesh):
    heads, ctx = mesh.shape["tensor"], mesh.shape["context"]

    def shards(tokens, w_query, w_key, w_value, mix_gate, mix_up, mix_down, block_ids):
        rows, depth = tokens.shape
        slab = rows // heads
        seq_rows = rows // SEQS
        tile = 16 if slab % 16 == 0 else slab
        mixf = mix_gate.shape[1]
        parts = 8
        dma = pltpu.SemaphoreType.DMA
        vmem = pl.BlockSpec(memory_space=pltpu.VMEM)
        hbm = pl.BlockSpec(memory_space=pltpu.HBM)
        return pl.pallas_call(
            functools.partial(kernel, heads, ctx, parts),
            out_shape=jax.ShapeDtypeStruct((rows, HEAD_DIM), BF16),
            in_specs=[hbm] * 8,
            out_specs=vmem,
            scratch_shapes=[
                pltpu.SMEM(block_ids.shape, jnp.int32),
                pltpu.VMEM(mix_gate.shape, BF16),
                pltpu.VMEM(mix_up.shape, BF16),
                pltpu.VMEM(mix_down.T.shape, BF16),
                pltpu.VMEM((rows, depth), BF16),
                pltpu.VMEM((depth, HEAD_DIM), BF16),
                pltpu.VMEM((depth, 2 * HEAD_DIM), BF16),
                pltpu.VMEM((2 * mixf * tile, heads * tile), BF16),
                pltpu.VMEM((heads * tile, mixf * tile), BF16),
                pltpu.VMEM((heads, slab, HEAD_DIM), BF16),
                pltpu.VMEM((heads, slab, HEAD_DIM), BF16),
                pltpu.VMEM((heads, slab, HEAD_DIM), BF16),
                pltpu.VMEM((ctx, heads, slab, HEAD_DIM), BF16),
                pltpu.VMEM((ctx, SEQS, seq_rows, HEAD_DIM), BF16),
                pltpu.VMEM((rows, HEAD_DIM), BF16),
                pltpu.VMEM((ctx, 8, 128), jnp.int32),
                pltpu.VMEM((SEQS, seq_rows, ctx * seq_rows), BF16),
                pltpu.VMEM((SEQS, seq_rows, HEAD_DIM), F32),
                dma((4 * parts + 4,)),
                dma((heads,)), dma((heads,)), dma((heads,)), dma((heads,)),
                dma((ctx,)), dma((ctx,)), dma((ctx,)), dma((ctx,)), dma((SEQS, ctx)), dma((SEQS, ctx)),
            ],
            compiler_params=pltpu.CompilerParams(
                collective_id=0, has_side_effects=True, vmem_limit_bytes=56 * 2**20
            ),
        )(block_ids, tokens, w_query, w_key, w_value, mix_gate, mix_up, mix_down.T)

    in_specs = (
        P("context", None),
        P(None, "tensor"),
        P(None, "tensor"),
        P(None, "tensor"),
        P(),
        P(),
        P(),
        P("context"),
    )
    out_specs = P("context", "tensor")
    return jax.shard_map(shards, mesh=mesh, in_specs=in_specs, out_specs=out_specs, check_vma=False)
```

```python
import functools

import jax
import jax.numpy as jnp
from jax import lax
from jax.experimental import pallas as pl
from jax.experimental.pallas import tpu as pltpu
from jax.sharding import PartitionSpec as P

HEAD_DIM = 128
BLK = 96
SEQS = 2
MESH = pl.DeviceIdType.MESH
F32 = jnp.float32
BF16 = jnp.bfloat16


def flat_rows(x):
    rows = x.size // x.shape[-1]
    if x.shape[-2] % 16:
        return x.astype(F32).reshape(rows, x.shape[-1]).astype(x.dtype)
    return x.reshape(rows, x.shape[-1])


def picks(shape, row_div, col_div):
    row = lax.broadcasted_iota(jnp.int32, shape, 0) // row_div
    col = lax.broadcasted_iota(jnp.int32, shape, 1) // col_div
    return (row == col).astype(F32)


def spread(small, step):
    tall, wide = small.shape[0] * step, small.shape[1] * step
    lifted = jnp.dot(
        picks((tall, small.shape[0]), step, 1), small, preferred_element_type=F32
    )
    lifted = jnp.dot(
        lifted, picks((small.shape[1], wide), 1, step), preferred_element_type=F32
    )
    row = lax.broadcasted_iota(jnp.int32, (tall, wide), 0) % step
    col = lax.broadcasted_iota(jnp.int32, (tall, wide), 1) % step
    return jnp.where(row == col, lifted, 0.0).astype(BF16)


def kernel(
    heads, ctx, parts,
    ids_hbm, x_ref, wq_ref, wk_ref, wv_ref, gate_hbm, up_hbm, down_hbm, out_ref,
    ids_ref, gate_ref, up_ref, down_ref,
    xbuf, wvbuf, wkqbuf, gubuf, dnbuf, vsend, vrecv, msend, mbuf, kbuf, qbuf, idbuf, pbuf, tbuf,
    load_sem, vs_sem, vr_sem, ms_sem, mr_sem, ks_sem, kr_sem, is_sem, ir_sem, cs_sem, cr_sem,
):
    ti = lax.axis_index("tensor")
    ci = lax.axis_index("context")
    rows, depth = x_ref.shape
    step = depth // parts
    slab = rows // heads
    seq_rows = rows // SEQS

    pairs = ctx // 2
    sib = ci + 1 - 2 * lax.rem(ci, 2)

    def far(d):
        return lax.rem(ci + 2 * d, ctx)

    def share(ref, peer, send, recv):
        copy = pltpu.make_async_remote_copy(
            src_ref=ref, dst_ref=ref, send_sem=send, recv_sem=recv,
            device_id={"context": peer}, device_id_type=MESH,
        )
        copy.start()
        return copy

    def arrived(ref, recv):
        pltpu.make_async_remote_copy(
            src_ref=ref, dst_ref=ref, send_sem=ks_sem.at[0], recv_sem=recv,
            device_id={"context": sib}, device_id_type=MESH,
        ).wait_recv()

    loads = []

    def load(src, dst):
        copy = pltpu.make_async_copy(src, dst, load_sem.at[len(loads)])
        copy.start()
        loads.append(copy)
        return copy

    small_loads = [
        load(gate_hbm, gate_ref), load(up_hbm, up_ref), load(down_hbm, down_ref), load(ids_hbm, ids_ref)
    ]
    v_loads, kq_loads = [], []
    for i in range(parts):
        ks = pl.ds(i * step, step)
        v_loads.append(
            (load(x_ref.at[:, ks], xbuf.at[:, ks]), load(wv_ref.at[ks, :], wvbuf.at[ks, :]))
        )

    def load_kq(i):
        ks = pl.ds(i * step, step)
        kq_loads.append(
            (
                load(wk_ref.at[ks, :], wkqbuf.at[ks, 0:HEAD_DIM]),
                load(wq_ref.at[ks, :], wkqbuf.at[ks, HEAD_DIM : 2 * HEAD_DIM]),
            )
        )

    barrier = pltpu.get_barrier_semaphore()
    for d in range(1, heads):
        pl.semaphore_signal(
            barrier, inc=1, device_id={"tensor": lax.rem(ti + d, heads)}, device_id_type=MESH
        )
    for d in range(1, ctx):
        pl.semaphore_signal(
            barrier, inc=1, device_id={"context": lax.rem(ci + d, ctx)}, device_id_type=MESH
        )

    for copy in small_loads:
        copy.wait()

    tile = 16 if slab % 16 == 0 else slab
    half = gate_ref.shape[1] * tile
    gubuf[0:half] = spread(gate_ref[...].astype(F32).T, tile)
    gubuf[half : 2 * half] = spread(up_ref[...].astype(F32).T, tile)
    dnbuf[...] = spread(down_ref[...].astype(F32), tile)

    sub = lax.broadcasted_iota(jnp.int32, (8, 128), 0)
    own_ids = jnp.zeros((8, 128), jnp.int32)
    for b in range(2 * SEQS):
        own_ids = jnp.where(sub == b, ids_ref[b], own_ids)
    idbuf[ci] = own_ids

    acc = jnp.zeros((rows, HEAD_DIM), F32)
    for i in range(parts):
        for copy in v_loads[i]:
            copy.wait()
        if i >= parts // 2:
            load_kq(2 * i - parts)
            load_kq(2 * i - parts + 1)
        ks = slice(i * step, (i + 1) * step)
        acc += jnp.dot(xbuf[:, ks], wvbuf[ks, :], preferred_element_type=F32)
    if slab % 16:
        vsend[...] = acc.reshape(heads, slab, HEAD_DIM).astype(BF16)
    else:
        vsend[...] = acc.astype(BF16).reshape(heads, slab, HEAD_DIM)

    pl.semaphore_wait(barrier, heads - 1 + ctx - 1)

    far_first = sorted(range(1, heads), key=lambda d: -min(d, heads - d))
    v_copies = []
    for d in far_first:
        peer = lax.rem(ti + d, heads)
        copy = pltpu.make_async_remote_copy(
            src_ref=vsend.at[peer], dst_ref=vrecv.at[ti],
            send_sem=vs_sem.at[d], recv_sem=vr_sem.at[ti],
            device_id={"tensor": peer}, device_id_type=MESH,
        )
        copy.start()
        v_copies.append(copy)
    i_copies = []
    for d in range(1, ctx):
        peer = lax.rem(ci + d, ctx)
        copy = pltpu.make_async_remote_copy(
            src_ref=idbuf.at[ci], dst_ref=idbuf.at[ci],
            send_sem=is_sem.at[d], recv_sem=ir_sem.at[ci],
            device_id={"context": peer}, device_id_type=MESH,
        )
        copy.start()
        i_copies.append(copy)
    vrecv[ti] = vsend[ti]

    acc = jnp.zeros((rows, 2 * HEAD_DIM), F32)
    for i in range(parts):
        for copy in kq_loads[i]:
            copy.wait()
        ks = slice(i * step, (i + 1) * step)
        acc += jnp.dot(xbuf[:, ks], wkqbuf[ks, :], preferred_element_type=F32)
    kbuf[ci] = acc[:, :HEAD_DIM].astype(BF16).reshape(SEQS, seq_rows, HEAD_DIM)
    k_copies = [share(kbuf.at[ci], sib, ks_sem.at[0], kr_sem.at[ci])]
    for d in range(1, pairs):
        k_copies.append(share(kbuf.at[ci], far(d), ks_sem.at[d], kr_sem.at[ci]))
    qbuf[...] = acc[:, HEAD_DIM:].astype(BF16)

    for d in range(1, heads):
        src = lax.rem(ti + d, heads)
        pltpu.make_async_remote_copy(
            src_ref=vsend.at[src], dst_ref=vrecv.at[src],
            send_sem=vs_sem.at[d], recv_sem=vr_sem.at[src],
            device_id={"tensor": src}, device_id_type=MESH,
        ).wait_recv()
    pieces = slab // tile
    x = jnp.concatenate(
        [flat_rows(vrecv[:, j * tile : (j + 1) * tile, :]) for j in range(pieces)], axis=1
    )
    both = jnp.dot(gubuf[...], x, preferred_element_type=F32)
    hidden = (jax.nn.silu(both[:half]) * both[half:]).astype(BF16)
    mixed = x.astype(F32) + jnp.dot(dnbuf[...], hidden, preferred_element_type=F32)
    for j in range(pieces):
        piece = mixed[:, j * HEAD_DIM : (j + 1) * HEAD_DIM]
        if tile % 16:
            piece = piece.reshape(heads, tile, HEAD_DIM).astype(BF16)
        else:
            piece = piece.astype(BF16).reshape(heads, tile, HEAD_DIM)
        msend[:, j * tile : (j + 1) * tile, :] = piece
    m_copies = []
    for d in far_first:
        peer = lax.rem(ti + d, heads)
        copy = pltpu.make_async_remote_copy(
            src_ref=msend.at[peer], dst_ref=mbuf.at[ci, ti],
            send_sem=ms_sem.at[d], recv_sem=mr_sem.at[ti],
            device_id={"tensor": peer}, device_id_type=MESH,
        )
        copy.start()
        m_copies.append(copy)
    mbuf[ci, ti] = msend[ti]

    for d in range(1, pairs):
        arrived(kbuf.at[far(d)], kr_sem.at[far(d)])
        k_copies.append(share(kbuf.at[far(d)], sib, ks_sem.at[pairs - 1 + d], kr_sem.at[far(d)]))

    per_seq = heads // SEQS
    first = ti // per_seq
    order = [first] + [lax.rem(first + s, SEQS) for s in range(1, SEQS)]
    halves = [pl.ds(s * per_seq, per_seq) for s in order]
    c_copies = []
    for k, s in enumerate(order):
        for i in range(per_seq):
            p = s * per_seq + i

            @pl.when(p != ti)
            def _(p=p):
                pltpu.make_async_remote_copy(
                    src_ref=msend.at[p], dst_ref=mbuf.at[ci, p],
                    send_sem=ms_sem.at[0], recv_sem=mr_sem.at[p],
                    device_id={"tensor": p}, device_id_type=MESH,
                ).wait_recv()

        own = mbuf.at[ci, halves[k]]
        for d in range(1, pairs):
            c_copies.append(share(own, far(d), cs_sem.at[k, d], cr_sem.at[k, ci]))
        c_copies.append(share(own, sib, cs_sem.at[k, 0], cr_sem.at[k, ci]))

    for d in range(1, ctx):
        src = lax.rem(ci + d, ctx)
        arrived(idbuf.at[src], ir_sem.at[src])
    arrived(kbuf.at[sib], kr_sem.at[sib])
    for d in range(1, pairs):
        there = lax.rem(sib + 2 * d, ctx)
        arrived(kbuf.at[there], kr_sem.at[there])
    scale = HEAD_DIM ** (-0.5)
    count = ctx * seq_rows
    lane = lax.broadcasted_iota(jnp.int32, (1, count), 1)
    row = lax.broadcasted_iota(jnp.int32, (seq_rows, 1), 0)
    for s in range(SEQS):
        key_pos = jnp.zeros((1, count), jnp.int32)
        for c in range(ctx):
            ids = idbuf[c]
            for b in range(2):
                r = 2 * s + b
                wide = jnp.concatenate([ids[r : r + 1, :]] * (count // 128), axis=1)
                key_pos = jnp.where(lane // BLK == 2 * c + b, wide, key_pos)
        key_pos = key_pos * BLK + lane % BLK
        query_pos = (
            jnp.where(row < BLK, ids_ref[2 * s], ids_ref[2 * s + 1]) * BLK + row % BLK
        )
        keys = kbuf[:, s].reshape(count, HEAD_DIM)
        scores = lax.dot_general(
            qbuf[s * seq_rows : (s + 1) * seq_rows, :], keys,
            (((1,), (1,)), ((), ())), preferred_element_type=F32,
        ) * scale
        scores = jnp.where(key_pos <= query_pos, scores, -1e30)
        weights = jnp.exp(scores - jnp.max(scores, axis=1, keepdims=True))
        tbuf[s] = jnp.broadcast_to(jnp.sum(weights, axis=1, keepdims=True), (seq_rows, HEAD_DIM))
        pbuf[s] = weights.astype(BF16)

    for k in range(SEQS):
        for d in range(1, pairs):
            got = mbuf.at[far(d), halves[k]]
            arrived(got, cr_sem.at[k, far(d)])
            c_copies.append(share(got, sib, cs_sem.at[k, pairs - 1 + d], cr_sem.at[k, far(d)]))
    for k, s in enumerate(order):
        arrived(mbuf.at[sib, halves[k]], cr_sem.at[k, sib])
        for d in range(1, pairs):
            there = lax.rem(sib + 2 * d, ctx)
            arrived(mbuf.at[there, halves[k]], cr_sem.at[k, there])
        values = flat_rows(mbuf[:, halves[k]])
        summed = jnp.dot(pbuf[s], values, preferred_element_type=F32)
        out_ref[pl.ds(pl.multiple_of(s * seq_rows, 16), seq_rows), :] = (summed / tbuf[s]).astype(BF16)

    for copy in v_copies + i_copies + k_copies + m_copies + c_copies:
        copy.wait_send()


def solution(mesh):
    heads, ctx = mesh.shape["tensor"], mesh.shape["context"]

    def shards(tokens, w_query, w_key, w_value, mix_gate, mix_up, mix_down, block_ids):
        rows, depth = tokens.shape
        slab = rows // heads
        seq_rows = rows // SEQS
        tile = 16 if slab % 16 == 0 else slab
        mixf = mix_gate.shape[1]
        parts = 8
        dma = pltpu.SemaphoreType.DMA
        vmem = pl.BlockSpec(memory_space=pltpu.VMEM)
        hbm = pl.BlockSpec(memory_space=pltpu.HBM)
        return pl.pallas_call(
            functools.partial(kernel, heads, ctx, parts),
            out_shape=pltpu.VMEM((rows, HEAD_DIM), BF16),
            in_specs=[hbm] * 8,
            out_specs=vmem,
            scratch_shapes=[
                pltpu.SMEM(block_ids.shape, jnp.int32),
                pltpu.VMEM(mix_gate.shape, BF16),
                pltpu.VMEM(mix_up.shape, BF16),
                pltpu.VMEM(mix_down.T.shape, BF16),
                pltpu.VMEM((rows, depth), BF16),
                pltpu.VMEM((depth, HEAD_DIM), BF16),
                pltpu.VMEM((depth, 2 * HEAD_DIM), BF16),
                pltpu.VMEM((2 * mixf * tile, heads * tile), BF16),
                pltpu.VMEM((heads * tile, mixf * tile), BF16),
                pltpu.VMEM((heads, slab, HEAD_DIM), BF16),
                pltpu.VMEM((heads, slab, HEAD_DIM), BF16),
                pltpu.VMEM((heads, slab, HEAD_DIM), BF16),
                pltpu.VMEM((ctx, heads, slab, HEAD_DIM), BF16),
                pltpu.VMEM((ctx, SEQS, seq_rows, HEAD_DIM), BF16),
                pltpu.VMEM((rows, HEAD_DIM), BF16),
                pltpu.VMEM((ctx, 8, 128), jnp.int32),
                pltpu.VMEM((SEQS, seq_rows, ctx * seq_rows), BF16),
                pltpu.VMEM((SEQS, seq_rows, HEAD_DIM), F32),
                dma((4 * parts + 4,)),
                dma((heads,)), dma((heads,)), dma((heads,)), dma((heads,)),
                dma((ctx,)), dma((ctx,)), dma((ctx,)), dma((ctx,)), dma((SEQS, ctx)), dma((SEQS, ctx)),
            ],
            compiler_params=pltpu.CompilerParams(
                collective_id=0, has_side_effects=True, vmem_limit_bytes=56 * 2**20
            ),
        )(block_ids, tokens, w_query, w_key, w_value, mix_gate, mix_up, mix_down.T)

    in_specs = (
        P("context", None),
        P(None, "tensor"),
        P(None, "tensor"),
        P(None, "tensor"),
        P(),
        P(),
        P(),
        P("context"),
    )
    out_specs = P("context", "tensor")
    return jax.shard_map(shards, mesh=mesh, in_specs=in_specs, out_specs=out_specs, check_vma=False)
```
